32 devices in a mesh: dp: 2 (over y), ulysses: 8 (over z, core), blk: 2 (over x).
Axes of the slice: x: 2, y: 2, z: 4, core: 2. Of those that a mesh axis runs over, the one named last changes fastest.
Arguments:
- tokens: bfloat16 [4, 1024, 1024], P('dp', ('ulysses', 'blk')), may hold values from -6 to 6
- norm_gain_attn: bfloat16 [1024], P(('dp', 'ulysses', 'blk')), may hold values from 0.5 to 1.5
- query_key_value_weight: bfloat16 [1024, 3072], P(('dp', 'ulysses', 'blk')), may hold values from -0.1875 to 0.1875
- attention_output_weight: bfloat16 [1024, 1024], P(('dp', 'ulysses', 'blk')), may hold values from -2 to 2
- norm_gain_mlp: bfloat16 [1024], P(('dp', 'ulysses', 'blk')), may hold values from 0.5 to 1.5
- input_projection_weight: bfloat16 [1024, 5248], P(('dp', 'ulysses', 'blk')), may hold values from -0.1875 to 0.1875
- down_projection_weight: bfloat16 [1024, 2624], P(('dp', 'ulysses', 'blk')), may hold values from -0.125 to 0.125
- cotangent: bfloat16 [4, 1024, 1024], P('dp', ('ulysses', 'blk')), may hold values from -6 to 6
Outputs:
- output: bfloat16 [4, 1024, 1024], P('dp', ('ulysses', 'blk'))
- input_grad: float32 [4, 1024, 1024], P('dp', ('ulysses', 'blk'))
- grad_norm_gain_attn: float32 [1024], P(('dp', 'ulysses', 'blk'))
- grad_qkv_weight: float32 [1024, 3072], P(('dp', 'ulysses', 'blk'))
- grad_out_weight: float32 [1024, 1024], P(('dp', 'ulysses', 'blk'))
- grad_norm_gain_mlp: float32 [1024], P(('dp', 'ulysses', 'blk'))
- grad_in_weight: float32 [1024, 5248], P(('dp', 'ulysses', 'blk'))
- grad_down_weight: float32 [1024, 2624], P(('dp', 'ulysses', 'blk'))
The draws below stay inside these ranges and needn't reach their ends.
All inputs are finite; a program needn't handle non-finite values.
Results may differ from the reference program's by a relative error of at most 0.023.
Values may be sent and summed in bfloat16 or wider, within the bound.
A program may use at most 256 MiB of HBM per device.

```python
import math
import jax
import jax.numpy as jnp
from jax import lax

D = 1024
FF = 2624
HEADS = 16
HEAD_DIM = 64
LEN = 1024
SEQS = 4


def with_spikes(entries, stream_key, source, target, shards_of, factor):
    owner, partner = [(jnp.arange(entries.shape[axis_at]) // (entries.shape[axis_at] // shards_of)).reshape([-1 if axis == axis_at else 1 for axis in range(entries.ndim)]) for axis_at in (source, target)]
    chosen = jax.random.permutation(stream_key, shards_of)[partner]
    strong = (owner == chosen) | (owner == (partner + shards_of // 2) % shards_of)
    return jnp.where(strong, factor * entries, entries)


def levels(rng, shape, shards, low, largest):
    def one(dim, blocks):
        steps = jax.random.uniform(jax.random.fold_in(jax.random.fold_in(rng, 6), dim), (blocks,), jnp.float32, low / len(shards), largest / len(shards))
        return jnp.repeat(jnp.exp(steps), shape[dim] // blocks).reshape((-1,) + (1,) * (len(shape) - dim - 1))

    level = one(*shards[0])
    for cut in shards[1:]:
        level = level * one(*cut)
    return level


def bell_draw(key, shape, scale, most, split=(), held_as=jnp.bfloat16):
    values = scale * jax.random.normal(key, shape, jnp.float32)
    if split:
        values = values * levels(key, shape, split, -0.22, 0.18)
    return jnp.clip(values, -most, most).astype(held_as)


def gaussian_with(stream_key, extent, spread, most, cuts, heavy, held_as=jnp.bfloat16):
    array = spread * jax.random.normal(stream_key, extent, jnp.float32)
    if cuts:
        array = array * levels(stream_key, extent, cuts, -0.22, 0.18)
    return jnp.clip(with_spikes(array, jax.random.fold_in(stream_key, 3), *heavy), -most, most).astype(held_as)


def setup_inputs(seed: int = 0) -> dict:
    streams_of = jax.random.split(jax.random.key(seed), 9)
    return {
        "tokens": bell_draw(streams_of[0], (SEQS, LEN, D), 1.0, 6.0, ((0, 2), (1, 16))),
        "norm_gain_attn": jnp.clip(1.0 + 0.1 * jax.random.normal(streams_of[1], (D,), jnp.float32), 0.5, 1.5).astype(jnp.bfloat16),
        "query_key_value_weight": bell_draw(streams_of[2], (D, 3 * D), D ** -0.5, 0.1875, ((0, 32),)),
        "attention_output_weight": bell_draw(streams_of[3], (D, D), (max(1, D * 8 // LEN)) ** -0.5, 2.0, ((0, 32),)),
        "norm_gain_mlp": jnp.clip(1.0 + 0.1 * jax.random.normal(streams_of[4], (D,), jnp.float32), 0.5, 1.5).astype(jnp.bfloat16),
        "input_projection_weight": bell_draw(streams_of[5], (D, 2 * FF), D ** -0.5, 0.1875, ((0, 32),)),
        "down_projection_weight": bell_draw(streams_of[6], (D, FF), FF ** -0.5, 0.125, ((0, 32),)),
        "cotangent": gaussian_with(streams_of[7], (SEQS, LEN, D), 1.0, 6.0, ((0, 2), (1, 16)), (1, 2, 16, 2.0)),
    }


EPSILON = 1e-05
ROPE_BASE = 160000.0

@jax.custom_vjp
def low(v):
    return lax.optimization_barrier(v.astype(jnp.bfloat16)).astype(jnp.float32)

@jax.custom_vjp
def low_back(v):
    return v

def low_keep(v):
    return (low(v), None)

def low_pass(kept, grad):
    return (grad,)

def back_keep(v):
    return (v, None)

def back_low(kept, grad):
    return (low(grad),)
low.defvjp(low_keep, low_pass)
low_back.defvjp(back_keep, back_low)

def layer_norm(values, gain):
    average = lax.optimization_barrier(jnp.mean(values, axis=-1, keepdims=True))
    centered = values - average
    variance = lax.optimization_barrier(jnp.mean(centered * centered, axis=-1, keepdims=True))
    return centered * lax.rsqrt(variance + EPSILON) * gain

def rope_tables(positions, half_dim):
    ladder = jnp.arange(half_dim, dtype=jnp.float32)
    frequency = ROPE_BASE ** (-2.0 * ladder / (2 * half_dim))
    angles = positions[:, None] * frequency[None, :]
    return (jnp.cos(angles)[:, None, :], jnp.sin(angles)[:, None, :])

def rotate(values, cosine, sine):
    half_dim = values.shape[-1] // 2
    first_half = values[..., :half_dim]
    second_half = values[..., half_dim:]
    return jnp.concatenate([first_half * cosine - second_half * sine, second_half * cosine + first_half * sine], axis=-1)

def attend(items):
    queries, keys, values = items
    highest = lax.Precision.HIGHEST
    scale_factor = 1.0 / math.sqrt(HEAD_DIM)
    scores = low_back(jnp.einsum('qhe,khe->hqk', queries, keys, precision=highest) * scale_factor)
    weights = jax.nn.softmax(scores, axis=-1)
    return jnp.einsum('hqk,khe->qhe', low(weights), values, precision=highest)

def forward(tokens, gain_attn, query_key_value_weight, attention_output_weight, gain_mlp, input_projection_weight, down_projection_weight):
    highest = lax.Precision.HIGHEST
    normed_attention_input = low(layer_norm(tokens, gain_attn))
    joined_heads = low(low_back(jnp.einsum('aqx,xt->aqt', normed_attention_input, query_key_value_weight, precision=highest)))
    joined_heads = joined_heads.reshape(SEQS, LEN, HEADS, 3, HEAD_DIM)
    cosine, sine = rope_tables(jnp.arange(LEN, dtype=jnp.float32), HEAD_DIM // 2)
    queries = low(rotate(joined_heads[:, :, :, 0, :], cosine, sine))
    keys = low(rotate(joined_heads[:, :, :, 1, :], cosine, sine))
    values = joined_heads[:, :, :, 2, :]
    attended_rows = lax.map(jax.checkpoint(attend), (queries, keys, values))
    attended_rows = low(low_back(attended_rows)).reshape(SEQS, LEN, HEADS * HEAD_DIM)
    middle_hidden = tokens + low_back(jnp.einsum('aqx,xt->aqt', attended_rows, attention_output_weight, precision=highest))
    normed_feedforward_input = low(layer_norm(middle_hidden, gain_mlp))
    hidden_input = low_back(jnp.einsum('aqx,xt->aqt', normed_feedforward_input, input_projection_weight, precision=highest))
    activated_half = low(jax.nn.gelu(hidden_input[..., :FF], approximate=False) * hidden_input[..., FF:])
    return middle_hidden + jnp.einsum('onf,bf->onb', activated_half, down_projection_weight, precision=highest)

def reference(tokens, norm_gain_attn, query_key_value_weight, attention_output_weight, norm_gain_mlp, input_projection_weight, down_projection_weight, cotangent):
    inputs = (tokens.astype(jnp.float32), norm_gain_attn.astype(jnp.float32), query_key_value_weight.astype(jnp.float32), attention_output_weight.astype(jnp.float32), norm_gain_mlp.astype(jnp.float32), input_projection_weight.astype(jnp.float32), down_projection_weight.astype(jnp.float32))
    result, pull = jax.vjp(forward, *inputs)
    grads = pull(cotangent.astype(jnp.float32))
    return (result.astype(jnp.bfloat16), grads[0], grads[1], grads[2], grads[3], grads[4], grads[5], grads[6])
```

```python
import math

import jax
import jax.numpy as jnp
from jax import lax
from jax.experimental import pallas as pl
from jax.experimental.pallas import tpu as pltpu
from jax.sharding import PartitionSpec as P

FF = 2624
HEADS = 16
HEAD_DIM = 64


EPSILON = 1e-05
ROPE_BASE = 160000.0


def layer_norm(values, gain):
    average = jnp.mean(values, axis=-1, keepdims=True)
    centered = values - average
    variance = jnp.mean(centered * centered, axis=-1, keepdims=True)
    return centered * lax.rsqrt(variance + EPSILON) * gain


def rope_tables(positions, half_dim):
    ladder = jnp.arange(half_dim, dtype=jnp.float32)
    frequency = ROPE_BASE ** (-2.0 * ladder / (2 * half_dim))
    angles = positions[:, None] * frequency[None, :]
    return (jnp.cos(angles)[:, None, :], jnp.sin(angles)[:, None, :])


def rotate(values, cosine, sine):
    half_dim = values.shape[-1] // 2
    first_half = values[..., :half_dim]
    second_half = values[..., half_dim:]
    return jnp.concatenate(
        [first_half * cosine - second_half * sine, second_half * cosine + first_half * sine],
        axis=-1,
    )


def rotate_back(gradient, cosine, sine):
    half_dim = gradient.shape[-1] // 2
    first_half = gradient[..., :half_dim]
    second_half = gradient[..., half_dim:]
    return jnp.concatenate(
        [first_half * cosine + second_half * sine, second_half * cosine - first_half * sine],
        axis=-1,
    )


def contract_rows(left_side, right_side):
    return lax.dot_general(
        left_side, right_side, (((0,), (0,)), ((), ())), preferred_element_type=jnp.float32
    )


def contract_cols(left_side, right_side):
    return lax.dot_general(
        left_side, right_side, (((1,), (1,)), ((), ())), preferred_element_type=jnp.float32
    )


BF = jnp.bfloat16
MESH = pl.DeviceIdType.MESH


def exchange(x, axes, cid):
    sizes = [lax.axis_size(a) for a in axes]
    n = math.prod(sizes)

    def kernel(x_ref, o_ref, send, recv, local):
        me = 0
        for a, s in zip(axes, sizes):
            me = me * s + lax.axis_index(a)

        def place(k):
            ids = {}
            for a, s in reversed(list(zip(axes, sizes))):
                ids[a] = lax.rem(k, s)
                k = k // s
            return ids

        barrier = pltpu.get_barrier_semaphore()
        for k in range(1, n):
            pl.semaphore_signal(
                barrier, 1, device_id=place(lax.rem(me + k, n)), device_id_type=MESH
            )
        pl.semaphore_wait(barrier, n - 1)
        copies = []
        for k in range(1, n):
            peer = lax.rem(me + k, n)
            copy = pltpu.make_async_remote_copy(
                src_ref=x_ref.at[peer],
                dst_ref=o_ref.at[me],
                send_sem=send.at[k],
                recv_sem=recv.at[k],
                device_id=place(peer),
                device_id_type=MESH,
            )
            copy.start()
            copies.append(copy)
        own = pltpu.make_async_copy(x_ref.at[me], o_ref.at[me], local)
        own.start()
        own.wait()
        for copy in copies:
            copy.wait()

    return pl.pallas_call(
        kernel,
        out_shape=jax.ShapeDtypeStruct(x.shape, x.dtype),
        in_specs=[pl.BlockSpec(memory_space=pl.ANY)],
        out_specs=pl.BlockSpec(memory_space=pl.ANY),
        scratch_shapes=[
            pltpu.SemaphoreType.DMA((n,)),
            pltpu.SemaphoreType.DMA((n,)),
            pltpu.SemaphoreType.DMA,
        ],
        compiler_params=pltpu.CompilerParams(collective_id=cid, has_side_effects=True),
    )(x)


def gather_line(x, cid):
    n = lax.axis_size("ulysses")
    chips = n // 2

    def kernel(x_ref, o_ref, send, recv, pass_send, pass_recv, local):
        me = lax.axis_index("ulysses")
        chip, core = me // 2, lax.rem(me, 2)
        partner = chip * 2 + (1 - core)
        barrier = pltpu.get_barrier_semaphore()
        pl.semaphore_signal(barrier, 1, device_id={"ulysses": partner}, device_id_type=MESH)
        for k in range(1, chips):
            peer = lax.rem(chip + k, chips) * 2 + core
            pl.semaphore_signal(barrier, 1, device_id={"ulysses": peer}, device_id_type=MESH)
        pl.semaphore_wait(barrier, chips)
        far = []
        for k in range(1, chips):
            peer = lax.rem(chip + k, chips) * 2 + core
            copy = pltpu.make_async_remote_copy(
                src_ref=x_ref,
                dst_ref=o_ref.at[me],
                send_sem=send.at[k],
                recv_sem=recv.at[k],
                device_id={"ulysses": peer},
                device_id_type=MESH,
            )
            copy.start()
            far.append(copy)
        near = [
            pltpu.make_async_remote_copy(
                src_ref=x_ref,
                dst_ref=o_ref.at[me],
                send_sem=pass_send.at[0],
                recv_sem=pass_recv.at[0],
                device_id={"ulysses": partner},
                device_id_type=MESH,
            )
        ]
        near[0].start()
        own = pltpu.make_async_copy(x_ref, o_ref.at[me], local)
        own.start()
        for k in range(1, chips):
            far[k - 1].wait_recv()
            slot = lax.rem(chip - k + chips, chips) * 2 + core
            copy = pltpu.make_async_remote_copy(
                src_ref=o_ref.at[slot],
                dst_ref=o_ref.at[slot],
                send_sem=pass_send.at[k],
                recv_sem=pass_recv.at[k],
                device_id={"ulysses": partner},
                device_id_type=MESH,
            )
            copy.start()
            near.append(copy)
        own.wait()
        for copy in far:
            copy.wait_send()
        for copy in near:
            copy.wait()

    return pl.pallas_call(
        kernel,
        out_shape=jax.ShapeDtypeStruct((n,) + x.shape, x.dtype),
        in_specs=[pl.BlockSpec(memory_space=pl.ANY)],
        out_specs=pl.BlockSpec(memory_space=pl.ANY),
        scratch_shapes=[pltpu.SemaphoreType.DMA((chips,))] * 4 + [pltpu.SemaphoreType.DMA],
        compiler_params=pltpu.CompilerParams(collective_id=cid, has_side_effects=True),
    )(x)


def scatter_line(x, cid):
    n, rows, cols = x.shape
    chips = n // 2

    def kernel(x_ref, o_ref, pair, summed, land, send, recv, pass_send, pass_recv):
        me = lax.axis_index("ulysses")
        chip, core = me // 2, lax.rem(me, 2)
        partner = chip * 2 + (1 - core)
        barrier = pltpu.get_barrier_semaphore()
        pl.semaphore_signal(barrier, 1, device_id={"ulysses": partner}, device_id_type=MESH)
        for k in range(1, chips):
            peer = lax.rem(chip + k, chips) * 2 + core
            pl.semaphore_signal(barrier, 1, device_id={"ulysses": peer}, device_id_type=MESH)
        pl.semaphore_wait(barrier, chips)
        order = list(range(1, chips)) + [0]
        near, far = {}, {}
        for k in order:
            there = lax.rem(chip + k, chips)
            near[k] = pltpu.make_async_remote_copy(
                src_ref=x_ref.at[there * 2 + (1 - core)],
                dst_ref=pair.at[k],
                send_sem=pass_send.at[k],
                recv_sem=pass_recv.at[k],
                device_id={"ulysses": partner},
                device_id_type=MESH,
            )
            near[k].start()
        for k in order:
            there = lax.rem(chip + k, chips)
            near[k].wait_recv()
            total = x_ref[there * 2 + core].astype(jnp.float32) + pair[k].astype(jnp.float32)
            if k == 0:
                o_ref[...] = total
            else:
                summed[k] = total.astype(BF)
                far[k] = pltpu.make_async_remote_copy(
                    src_ref=summed.at[k],
                    dst_ref=land.at[k],
                    send_sem=send.at[k],
                    recv_sem=recv.at[k],
                    device_id={"ulysses": there * 2 + core},
                    device_id_type=MESH,
                )
                far[k].start()
        for k in range(1, chips):
            far[k].wait_recv()
            o_ref[...] += land[k].astype(jnp.float32)
        for k in order:
            near[k].wait_send()
            if k:
                far[k].wait_send()

    block = pltpu.VMEM((chips, rows, cols), BF)
    return pl.pallas_call(
        kernel,
        out_shape=jax.ShapeDtypeStruct((rows, cols), jnp.float32),
        in_specs=[pl.BlockSpec(memory_space=pltpu.VMEM)],
        out_specs=pl.BlockSpec(memory_space=pltpu.VMEM),
        scratch_shapes=[block] * 3 + [pltpu.SemaphoreType.DMA((chips,))] * 4,
        compiler_params=pltpu.CompilerParams(
            collective_id=cid, has_side_effects=True, vmem_limit_bytes=40 * 1024 * 1024
        ),
    )(x)


def pad_to(x, cols):
    return jnp.pad(x, [(0, 0)] * (x.ndim - 1) + [(0, cols - x.shape[-1])])


def body(
    tokens,
    norm_gain_attn,
    query_key_value_weight,
    attention_output_weight,
    norm_gain_mlp,
    input_projection_weight,
    down_projection_weight,
    cotangent,
):
    seq_count, local_len, width = tokens.shape
    n_dp, n_u, n_b = (lax.axis_size(a) for a in ("dp", "ulysses", "blk"))
    part = width // (n_dp * n_u * n_b)
    heads = HEADS // n_u
    head_cols = heads * 3 * HEAD_DIM
    ff_cols = FF // n_u
    ff_pad = -(-ff_cols // 128) * 128
    rows = seq_count * local_len
    length = rows * n_u
    f32 = jnp.float32

    qkv_cut = query_key_value_weight.reshape(part, n_u, head_cols).transpose(1, 0, 2)
    gains = jnp.stack([norm_gain_attn, norm_gain_mlp], axis=1)
    gains = jnp.broadcast_to(pad_to(gains, 128)[None], (n_u, part, 128))
    first_cut = jnp.concatenate([qkv_cut, gains], axis=2)
    in_cut = pad_to(input_projection_weight.reshape(part, 2, n_u, ff_cols), ff_pad)
    in_cut = in_cut.transpose(2, 0, 1, 3).reshape(n_u, part, 2 * ff_pad)
    down_cut = pad_to(down_projection_weight.reshape(part, n_u, ff_cols), ff_pad)
    mlp_cut = jnp.concatenate([in_cut, down_cut.transpose(1, 0, 2)], axis=2)

    def in_order(gathered):
        cols = gathered.shape[-1]
        gathered = gathered.reshape(n_dp, n_b, n_u, part, cols)
        return gathered.transpose(0, 2, 1, 3, 4).reshape(width, cols)

    def by_owner(grads):
        cols = grads.shape[-1]
        grads = grads.reshape(n_dp, n_u, n_b, part, cols).transpose(0, 2, 1, 3, 4)
        return grads.reshape(n_dp * n_b, n_u * part, cols)

    first_cut = exchange(first_cut, ("ulysses",), 1)
    mlp_cut = lax.all_to_all(mlp_cut, "ulysses", 0, 0)
    mlp_full = in_order(
        lax.all_gather(mlp_cut.reshape(n_u * part, -1), ("dp", "blk"), axis=0, tiled=True)
    )
    out_full = lax.all_gather(
        attention_output_weight, ("dp", "ulysses", "blk"), axis=0, tiled=True
    )
    copies = jnp.broadcast_to(
        first_cut.reshape(1, n_u * part, -1), (n_dp * n_b, n_u * part, head_cols + 128)
    )
    first_full = in_order(exchange(copies, ("dp", "blk"), 2))
    qkv_w = first_full[:, :head_cols]
    gain_attn_f = first_full[:, head_cols].astype(f32)
    gain_mlp_f = first_full[:, head_cols + 1].astype(f32)
    in_w = mlp_full[:, : 2 * ff_pad]
    down_w = mlp_full[:, 2 * ff_pad :]

    both = exchange(jnp.stack([tokens, cotangent], axis=1), ("blk",), 3)
    inputs_low = both[:, 0].reshape(rows, width)
    grad_top = both[:, 1].reshape(rows, width)
    inputs = inputs_low.astype(f32)
    tokens_all = gather_line(inputs_low, 4).reshape(length, width)
    cot_all = lax.all_gather(grad_top, "ulysses", axis=0, tiled=True)
    normed = layer_norm(tokens_all.astype(f32), gain_attn_f).astype(BF)
    joined = jnp.dot(normed, qkv_w, preferred_element_type=f32).astype(BF)
    joined = joined.reshape(length, heads, 3 * HEAD_DIM)
    cosine, sine = rope_tables(jnp.arange(length, dtype=f32), HEAD_DIM // 2)
    queries = rotate(joined[..., :HEAD_DIM].astype(f32), cosine, sine).astype(BF)
    keys = rotate(joined[..., HEAD_DIM : 2 * HEAD_DIM].astype(f32), cosine, sine).astype(BF)
    queries, keys = queries.transpose(1, 0, 2), keys.transpose(1, 0, 2)
    values = joined[..., 2 * HEAD_DIM :].transpose(1, 0, 2)
    scale = 1.0 / math.sqrt(HEAD_DIM)

    def probs_of(queries, keys):
        scores = jnp.einsum("hqe,hke->hqk", queries, keys, preferred_element_type=f32) * scale
        exponent = jnp.exp(scores - jnp.max(scores, axis=-1, keepdims=True))
        return exponent / jnp.sum(exponent, axis=-1, keepdims=True)

    weights = probs_of(queries, keys)
    probs = weights.astype(BF)
    attended = jnp.einsum("hqk,hke->qhe", probs, values, preferred_element_type=f32)
    attended = attended.astype(BF).reshape(n_u, rows, heads * HEAD_DIM)
    back = exchange(attended, ("ulysses",), 5).transpose(1, 0, 2).reshape(rows, width)

    middle = inputs + jnp.dot(back, out_full, preferred_element_type=f32)
    normed_mlp_own = layer_norm(middle, gain_mlp_f).astype(BF)
    normed_mlp = gather_line(normed_mlp_own, 6).reshape(length, width)
    hidden = jnp.dot(normed_mlp, in_w, preferred_element_type=f32)

    def gated(hidden):
        return jax.nn.gelu(hidden[:, :ff_pad], approximate=False) * hidden[:, ff_pad:]

    active, gated_pull = jax.vjp(gated, hidden)
    active = active.astype(BF)
    grad_active = jnp.dot(cot_all, down_w, preferred_element_type=f32)
    grad_hidden = gated_pull(grad_active)[0].astype(BF)
    grad_normed = contract_cols(grad_hidden, in_w).astype(BF)
    grad_normed = scatter_line(grad_normed.reshape(n_u, rows, width), 7)
    mlp_part = contract_cols(active, down_w).astype(BF)
    mlp_sum = lax.psum_scatter(mlp_part, "ulysses", scatter_dimension=0, tiled=True)
    grad_in = contract_rows(normed_mlp, grad_hidden)
    grad_down = contract_rows(cot_all, active)
    mlp_grads = jnp.concatenate([grad_in, grad_down], axis=1).astype(BF)
    mlp_grads = lax.psum_scatter(
        by_owner(mlp_grads).reshape(width, -1), ("dp", "blk"), scatter_dimension=0, tiled=True
    )

    _, norm_pull = jax.vjp(layer_norm, middle, gain_mlp_f)
    grad_middle, gain_mlp_part = norm_pull(grad_normed)
    grad_middle = grad_top.astype(f32) + grad_middle
    grad_branch = grad_middle.astype(BF)
    grad_back = contract_cols(grad_branch, out_full).astype(BF)
    grad_back = grad_back.reshape(rows, n_u, heads * HEAD_DIM).transpose(1, 0, 2)
    grad_heads = exchange(grad_back, ("ulysses",), 8).reshape(length, heads, HEAD_DIM)
    grad_heads = grad_heads.transpose(1, 0, 2)
    grad_out = lax.psum_scatter(
        contract_rows(back, grad_branch).astype(BF),
        ("dp", "ulysses", "blk"),
        scatter_dimension=0,
        tiled=True,
    ).astype(f32)

    grad_values = jnp.einsum("hqk,hqe->khe", probs, grad_heads, preferred_element_type=f32)
    grad_probs = jnp.einsum("hqe,hke->hqk", grad_heads, values, preferred_element_type=f32)
    inner = jnp.sum(weights * grad_probs, axis=-1, keepdims=True)
    grad_scores = (weights * (grad_probs - inner)).astype(BF)
    grad_q = jnp.einsum("hqk,hke->qhe", grad_scores, keys, preferred_element_type=f32) * scale
    grad_k = jnp.einsum("hqk,hqe->khe", grad_scores, queries, preferred_element_type=f32) * scale
    grad_joined = jnp.concatenate(
        [rotate_back(grad_q, cosine, sine), rotate_back(grad_k, cosine, sine), grad_values],
        axis=-1,
    )
    grad_joined = grad_joined.astype(BF).reshape(length, head_cols)
    grad_first = contract_cols(grad_joined, qkv_w).astype(BF)
    grad_first = scatter_line(grad_first.reshape(n_u, rows, width), 9)
    _, first_pull = jax.vjp(layer_norm, inputs, gain_attn_f)
    grad_input, gain_attn_part = first_pull(grad_first)
    input_grad = grad_middle + grad_input
    output = middle + mlp_sum.astype(f32)
    ends = jnp.stack([output.astype(BF), input_grad.astype(BF)], axis=0)
    ends = ends.reshape(2, seq_count, local_len, width).transpose(1, 0, 2, 3)
    ends = exchange(ends, ("blk",), 10)
    output, input_grad = ends[:, 0], ends[:, 1].astype(f32)

    gain_parts = pad_to(jnp.stack([gain_attn_part, gain_mlp_part], axis=1), 128)
    first_grads = jnp.concatenate([contract_rows(normed, grad_joined), gain_parts], axis=1)
    first_grads = exchange(by_owner(first_grads.astype(BF)), ("dp", "blk"), 11)
    first_grads = jnp.sum(first_grads.astype(f32), axis=0).astype(BF)
    last = jnp.concatenate([first_grads, mlp_grads], axis=1).reshape(n_u, part, -1)
    last = exchange(last, ("ulysses",), 12)
    gain_sums = jnp.sum(last[:, :, head_cols : head_cols + 2].astype(f32), axis=0)
    grad_qkv = last[:, :, :head_cols].transpose(1, 0, 2).reshape(part, -1).astype(f32)
    at = head_cols + 128
    grad_in = last[:, :, at : at + 2 * ff_pad].reshape(n_u, part, 2, ff_pad)[..., :ff_cols]
    grad_in = grad_in.transpose(1, 2, 0, 3).reshape(part, -1).astype(f32)
    grad_down = last[:, :, at + 2 * ff_pad :][..., :ff_cols]
    grad_down = grad_down.transpose(1, 0, 2).reshape(part, -1).astype(f32)
    return (
        output,
        input_grad,
        gain_sums[:, 0],
        grad_qkv,
        grad_out,
        gain_sums[:, 1],
        grad_in,
        grad_down,
    )


def solution(mesh):
    in_specs = (
        P("dp", ("ulysses", "blk"), None),
        P(("dp", "ulysses", "blk")),
        P(("dp", "ulysses", "blk"), None),
        P(("dp", "ulysses", "blk"), None),
        P(("dp", "ulysses", "blk")),
        P(("dp", "ulysses", "blk"), None),
        P(("dp", "ulysses", "blk"), None),
        P("dp", ("ulysses", "blk"), None),
    )
    out_specs = (
        P("dp", ("ulysses", "blk"), None),
        P("dp", ("ulysses", "blk"), None),
        P(("dp", "ulysses", "blk")),
        P(("dp", "ulysses", "blk"), None),
        P(("dp", "ulysses", "blk"), None),
        P(("dp", "ulysses", "blk")),
        P(("dp", "ulysses", "blk"), None),
        P(("dp", "ulysses", "blk"), None),
    )
    return jax.shard_map(body, mesh=mesh, in_specs=in_specs, out_specs=out_specs, check_vma=False)
```

```python
import math

import jax
import jax.numpy as jnp
from jax import lax
from jax.experimental import pallas as pl
from jax.experimental.pallas import tpu as pltpu
from jax.sharding import PartitionSpec as P

FF = 2624
HEADS = 16
HEAD_DIM = 64


EPSILON = 1e-05
ROPE_BASE = 160000.0


def layer_norm(values, gain):
    average = jnp.mean(values, axis=-1, keepdims=True)
    centered = values - average
    variance = jnp.mean(centered * centered, axis=-1, keepdims=True)
    return centered * lax.rsqrt(variance + EPSILON) * gain


def rope_tables(positions, half_dim):
    ladder = jnp.arange(half_dim, dtype=jnp.float32)
    frequency = ROPE_BASE ** (-2.0 * ladder / (2 * half_dim))
    angles = positions[:, None] * frequency[None, :]
    return (jnp.cos(angles)[:, None, :], jnp.sin(angles)[:, None, :])


def rotate(values, cosine, sine):
    half_dim = values.shape[-1] // 2
    first_half = values[..., :half_dim]
    second_half = values[..., half_dim:]
    return jnp.concatenate(
        [first_half * cosine - second_half * sine, second_half * cosine + first_half * sine],
        axis=-1,
    )


def rotate_back(gradient, cosine, sine):
    half_dim = gradient.shape[-1] // 2
    first_half = gradient[..., :half_dim]
    second_half = gradient[..., half_dim:]
    return jnp.concatenate(
        [first_half * cosine + second_half * sine, second_half * cosine - first_half * sine],
        axis=-1,
    )


def contract_rows(left_side, right_side):
    return lax.dot_general(
        left_side, right_side, (((0,), (0,)), ((), ())), preferred_element_type=jnp.float32
    )


def contract_cols(left_side, right_side):
    return lax.dot_general(
        left_side, right_side, (((1,), (1,)), ((), ())), preferred_element_type=jnp.float32
    )


BF = jnp.bfloat16
MESH = pl.DeviceIdType.MESH


def together(ops, cid):
    n_u = lax.axis_size("ulysses")
    counts = []
    shapes = []
    for kind, x, axes in ops:
        n = n_u if kind == "line" else math.prod(lax.axis_size(a) for a in axes)
        counts.append(n)
        shape = x.shape if kind == "swap" else (n,) + x.shape
        shapes.append(jax.ShapeDtypeStruct(shape, x.dtype))
    many = len(ops)

    def kernel(*refs):
        sources, results, sems = refs[:many], refs[many : 2 * many], refs[2 * many :]
        barrier = pltpu.get_barrier_semaphore()
        plans = []
        expected = 0
        for (kind, _, axes), n in zip(ops, counts):
            if kind == "line":
                me = lax.axis_index("ulysses")
                chip, core = me // 2, lax.rem(me, 2)
                peers = [chip * 2 + (1 - core)]
                peers += [lax.rem(chip + k, n // 2) * 2 + core for k in range(1, n // 2)]
                places = [{"ulysses": peer} for peer in peers]
            else:
                me = 0
                for a in axes:
                    me = me * lax.axis_size(a) + lax.axis_index(a)
                peers = [lax.rem(me + k, n) for k in range(1, n)]
                places = []
                for peer in peers:
                    ids = {}
                    for a in reversed(axes):
                        ids[a] = lax.rem(peer, lax.axis_size(a))
                        peer = peer // lax.axis_size(a)
                    places.append(ids)
            for ids in places:
                pl.semaphore_signal(barrier, 1, device_id=ids, device_id_type=MESH)
            expected += len(places)
            plans.append((me, peers, places))
        pl.semaphore_wait(barrier, expected)

        def remote(source, target, send, recv, ids):
            copy = pltpu.make_async_remote_copy(
                src_ref=source,
                dst_ref=target,
                send_sem=send,
                recv_sem=recv,
                device_id=ids,
                device_id_type=MESH,
            )
            copy.start()
            return copy

        started, local = [], []
        for i, (kind, _, _) in enumerate(ops):
            me, peers, places = plans[i]
            source, result = sources[i], results[i]
            send, recv, own = sems[3 * i : 3 * i + 3]
            copies = []
            for j in range(len(peers)):
                part = source.at[peers[j]] if kind == "swap" else source
                copies.append(remote(part, result.at[me], send.at[j], recv.at[j], places[j]))
            started.append(copies)
            part = source.at[me] if kind == "swap" else source
            local.append(pltpu.make_async_copy(part, result.at[me], own))
            local[-1].start()
        passed = []
        for i, (kind, _, _) in enumerate(ops):
            if kind != "line":
                continue
            me, _, places = plans[i]
            chips = counts[i] // 2
            chip, core = me // 2, lax.rem(me, 2)
            send, recv, _ = sems[3 * i : 3 * i + 3]
            for k in range(1, chips):
                started[i][k].wait_recv()
                slot = results[i].at[lax.rem(chip - k + chips, chips) * 2 + core]
                at = chips + k - 1
                passed.append(remote(slot, slot, send.at[at], recv.at[at], places[0]))
        for i, (kind, _, _) in enumerate(ops):
            for j, copy in enumerate(started[i]):
                if kind == "line" and j:
                    copy.wait_send()
                else:
                    copy.wait()
            local[i].wait()
        for copy in passed:
            copy.wait()

    scratch = []
    for n in counts:
        scratch += [pltpu.SemaphoreType.DMA((n,))] * 2 + [pltpu.SemaphoreType.DMA]
    return pl.pallas_call(
        kernel,
        out_shape=shapes,
        in_specs=[pl.BlockSpec(memory_space=pl.ANY)] * many,
        out_specs=[pl.BlockSpec(memory_space=pl.ANY)] * many,
        scratch_shapes=scratch,
        compiler_params=pltpu.CompilerParams(collective_id=cid, has_side_effects=True),
    )(*[x for _, x, _ in ops])


def scatter_line(x, cid):
    n, rows, cols = x.shape
    chips = n // 2

    def kernel(x_ref, o_ref, pair, summed, land, send, recv, pass_send, pass_recv):
        me = lax.axis_index("ulysses")
        chip, core = me // 2, lax.rem(me, 2)
        partner = chip * 2 + (1 - core)
        barrier = pltpu.get_barrier_semaphore()
        pl.semaphore_signal(barrier, 1, device_id={"ulysses": partner}, device_id_type=MESH)
        for k in range(1, chips):
            peer = lax.rem(chip + k, chips) * 2 + core
            pl.semaphore_signal(barrier, 1, device_id={"ulysses": peer}, device_id_type=MESH)
        pl.semaphore_wait(barrier, chips)
        order = list(range(1, chips)) + [0]
        near, far = {}, {}
        for k in order:
            there = lax.rem(chip + k, chips)
            near[k] = pltpu.make_async_remote_copy(
                src_ref=x_ref.at[there * 2 + (1 - core)],
                dst_ref=pair.at[k],
                send_sem=pass_send.at[k],
                recv_sem=pass_recv.at[k],
                device_id={"ulysses": partner},
                device_id_type=MESH,
            )
            near[k].start()
        for k in order:
            there = lax.rem(chip + k, chips)
            near[k].wait_recv()
            total = x_ref[there * 2 + core].astype(jnp.float32) + pair[k].astype(jnp.float32)
            if k == 0:
                o_ref[...] = total
            else:
                summed[k] = total.astype(BF)
                far[k] = pltpu.make_async_remote_copy(
                    src_ref=summed.at[k],
                    dst_ref=land.at[k],
                    send_sem=send.at[k],
                    recv_sem=recv.at[k],
                    device_id={"ulysses": there * 2 + core},
                    device_id_type=MESH,
                )
                far[k].start()
        for k in range(1, chips):
            far[k].wait_recv()
            o_ref[...] += land[k].astype(jnp.float32)
        for k in order:
            near[k].wait_send()
            if k:
                far[k].wait_send()

    block = pltpu.VMEM((chips, rows, cols), BF)
    return pl.pallas_call(
        kernel,
        out_shape=jax.ShapeDtypeStruct((rows, cols), jnp.float32),
        in_specs=[pl.BlockSpec(memory_space=pltpu.VMEM)],
        out_specs=pl.BlockSpec(memory_space=pltpu.VMEM),
        scratch_shapes=[block] * 3 + [pltpu.SemaphoreType.DMA((chips,))] * 4,
        compiler_params=pltpu.CompilerParams(
            collective_id=cid, has_side_effects=True, vmem_limit_bytes=40 * 1024 * 1024
        ),
    )(x)


def pad_to(x, cols):
    return jnp.pad(x, [(0, 0)] * (x.ndim - 1) + [(0, cols - x.shape[-1])])


def body(
    tokens,
    norm_gain_attn,
    query_key_value_weight,
    attention_output_weight,
    norm_gain_mlp,
    input_projection_weight,
    down_projection_weight,
    cotangent,
):
    seq_count, local_len, width = tokens.shape
    n_dp, n_u, n_b = (lax.axis_size(a) for a in ("dp", "ulysses", "blk"))
    part = width // (n_dp * n_u * n_b)
    heads = HEADS // n_u
    head_cols = heads * 3 * HEAD_DIM
    ff_cols = FF // n_u
    ff_pad = -(-ff_cols // 128) * 128
    rows = seq_count * local_len
    length = rows * n_u
    f32 = jnp.float32

    qkv_cut = query_key_value_weight.reshape(part, n_u, head_cols).transpose(1, 0, 2)
    gains = jnp.stack([norm_gain_attn, norm_gain_mlp], axis=1)
    gains = jnp.broadcast_to(pad_to(gains, 128)[None], (n_u, part, 128))
    first_cut = jnp.concatenate([qkv_cut, gains], axis=2)
    in_cut = pad_to(input_projection_weight.reshape(part, 2, n_u, ff_cols), ff_pad)
    in_cut = in_cut.transpose(2, 0, 1, 3).reshape(n_u, part, 2 * ff_pad)
    down_cut = pad_to(down_projection_weight.reshape(part, n_u, ff_cols), ff_pad)
    mlp_cut = jnp.concatenate([in_cut, down_cut.transpose(1, 0, 2)], axis=2)

    def in_order(gathered):
        cols = gathered.shape[-1]
        gathered = gathered.reshape(n_dp, n_b, n_u, part, cols)
        return gathered.transpose(0, 2, 1, 3, 4).reshape(width, cols)

    def by_owner(grads):
        cols = grads.shape[-1]
        grads = grads.reshape(n_dp, n_u, n_b, part, cols).transpose(0, 2, 1, 3, 4)
        return grads.reshape(n_dp * n_b, n_u * part, cols)

    both, first_cut, mlp_cut = together(
        [
            ("swap", jnp.stack([tokens, cotangent], axis=1), ("blk",)),
            ("swap", first_cut, ("ulysses",)),
            ("swap", mlp_cut, ("ulysses",)),
        ],
        1,
    )
    inputs_low = both[:, 0].reshape(rows, width)
    grad_top = both[:, 1].reshape(rows, width)
    first_full, tokens_all = together(
        [
            ("copy", first_cut.reshape(n_u * part, -1), ("dp", "blk")),
            ("line", inputs_low, None),
        ],
        2,
    )
    mlp_full = in_order(
        lax.all_gather(mlp_cut.reshape(n_u * part, -1), ("dp", "blk"), axis=0, tiled=True)
    )
    out_full = lax.all_gather(
        attention_output_weight, ("dp", "ulysses", "blk"), axis=0, tiled=True
    )
    first_full = in_order(first_full)
    qkv_w = first_full[:, :head_cols]
    gain_attn_f = first_full[:, head_cols].astype(f32)
    gain_mlp_f = first_full[:, head_cols + 1].astype(f32)
    in_w = mlp_full[:, : 2 * ff_pad]
    down_w = mlp_full[:, 2 * ff_pad :]

    inputs = inputs_low.astype(f32)
    tokens_all = tokens_all.reshape(length, width)
    cot_all = lax.all_gather(grad_top, "ulysses", axis=0, tiled=True)
    normed = layer_norm(tokens_all.astype(f32), gain_attn_f).astype(BF)
    joined = jnp.dot(normed, qkv_w, preferred_element_type=f32).astype(BF)
    joined = joined.reshape(length, heads, 3 * HEAD_DIM)
    cosine, sine = rope_tables(jnp.arange(length, dtype=f32), HEAD_DIM // 2)
    queries = rotate(joined[..., :HEAD_DIM].astype(f32), cosine, sine).astype(BF)
    keys = rotate(joined[..., HEAD_DIM : 2 * HEAD_DIM].astype(f32), cosine, sine).astype(BF)
    queries, keys = queries.transpose(1, 0, 2), keys.transpose(1, 0, 2)
    values = joined[..., 2 * HEAD_DIM :].transpose(1, 0, 2)
    scale = 1.0 / math.sqrt(HEAD_DIM)

    def probs_of(queries, keys):
        scores = jnp.einsum("hqe,hke->hqk", queries, keys, preferred_element_type=f32) * scale
        exponent = jnp.exp(scores - jnp.max(scores, axis=-1, keepdims=True))
        return exponent / jnp.sum(exponent, axis=-1, keepdims=True)

    weights = probs_of(queries, keys)
    probs = weights.astype(BF)
    attended = jnp.einsum("hqk,hke->qhe", probs, values, preferred_element_type=f32)
    attended = attended.astype(BF).reshape(n_u, rows, heads * HEAD_DIM)
    (back,) = together([("swap", attended, ("ulysses",))], 5)
    back = back.transpose(1, 0, 2).reshape(rows, width)

    middle = inputs + jnp.dot(back, out_full, preferred_element_type=f32)
    normed_mlp_own = layer_norm(middle, gain_mlp_f).astype(BF)
    (normed_mlp,) = together([("line", normed_mlp_own, None)], 6)
    normed_mlp = normed_mlp.reshape(length, width)
    hidden = jnp.dot(normed_mlp, in_w, preferred_element_type=f32)

    def gated(hidden):
        return jax.nn.gelu(hidden[:, :ff_pad], approximate=False) * hidden[:, ff_pad:]

    active, gated_pull = jax.vjp(gated, hidden)
    active = active.astype(BF)
    grad_active = jnp.dot(cot_all, down_w, preferred_element_type=f32)
    grad_hidden = gated_pull(grad_active)[0].astype(BF)
    grad_normed = contract_cols(grad_hidden, in_w).astype(BF)
    grad_normed = scatter_line(grad_normed.reshape(n_u, rows, width), 7)
    mlp_part = contract_cols(active, down_w).astype(BF)
    mlp_sum = lax.psum_scatter(mlp_part, "ulysses", scatter_dimension=0, tiled=True)
    grad_in = contract_rows(normed_mlp, grad_hidden)
    grad_down = contract_rows(cot_all, active)
    mlp_grads = jnp.concatenate([grad_in, grad_down], axis=1).astype(BF)
    mlp_grads = lax.psum_scatter(
        by_owner(mlp_grads).reshape(width, -1), ("dp", "blk"), scatter_dimension=0, tiled=True
    )

    _, norm_pull = jax.vjp(layer_norm, middle, gain_mlp_f)
    grad_middle, gain_mlp_part = norm_pull(grad_normed)
    grad_middle = grad_top.astype(f32) + grad_middle
    grad_branch = grad_middle.astype(BF)
    grad_back = contract_cols(grad_branch, out_full).astype(BF)
    grad_back = grad_back.reshape(rows, n_u, heads * HEAD_DIM).transpose(1, 0, 2)
    (grad_heads,) = together([("swap", grad_back, ("ulysses",))], 8)
    grad_heads = grad_heads.reshape(length, heads, HEAD_DIM).transpose(1, 0, 2)
    branch_all = lax.all_gather(grad_branch, "ulysses", axis=0, tiled=True)
    grad_out = contract_rows(attended.reshape(length, heads * HEAD_DIM), branch_all)
    grad_out = grad_out.astype(BF).reshape(n_dp * n_b, part, width)

    grad_values = jnp.einsum("hqk,hqe->khe", probs, grad_heads, preferred_element_type=f32)
    grad_probs = jnp.einsum("hqe,hke->hqk", grad_heads, values, preferred_element_type=f32)
    inner = jnp.sum(weights * grad_probs, axis=-1, keepdims=True)
    grad_scores = (weights * (grad_probs - inner)).astype(BF)
    grad_q = jnp.einsum("hqk,hke->qhe", grad_scores, keys, preferred_element_type=f32) * scale
    grad_k = jnp.einsum("hqk,hqe->khe", grad_scores, queries, preferred_element_type=f32) * scale
    grad_joined = jnp.concatenate(
        [rotate_back(grad_q, cosine, sine), rotate_back(grad_k, cosine, sine), grad_values],
        axis=-1,
    )
    grad_joined = grad_joined.astype(BF).reshape(length, head_cols)
    grad_first = contract_cols(grad_joined, qkv_w).astype(BF)
    grad_first = scatter_line(grad_first.reshape(n_u, rows, width), 9)
    _, first_pull = jax.vjp(layer_norm, inputs, gain_attn_f)
    grad_input, gain_attn_part = first_pull(grad_first)
    input_grad = grad_middle + grad_input
    output = middle + mlp_sum.astype(f32)
    ends = jnp.stack([output.astype(BF), input_grad.astype(BF)], axis=0)
    ends = ends.reshape(2, seq_count, local_len, width).transpose(1, 0, 2, 3)
    gain_parts = pad_to(jnp.stack([gain_attn_part, gain_mlp_part], axis=1), 128)
    first_grads = jnp.concatenate([contract_rows(normed, grad_joined), gain_parts], axis=1)
    ends, first_grads, grad_out, last_mlp = together(
        [
            ("swap", ends, ("blk",)),
            ("swap", by_owner(first_grads.astype(BF)), ("dp", "blk")),
            ("swap", grad_out, ("dp", "blk")),
            ("swap", mlp_grads.reshape(n_u, part, -1), ("ulysses",)),
        ],
        10,
    )
    output, input_grad = ends[:, 0], ends[:, 1].astype(f32)
    owners = [
        ((d * n_u + u) * n_b + b, u * n_dp * n_b + d * n_b + b)
        for d in range(n_dp)
        for u in range(n_u)
        for b in range(n_b)
    ]
    grad_out = jnp.sum(grad_out.astype(f32), axis=0).astype(BF)
    grad_out = lax.ppermute(grad_out, ("dp", "ulysses", "blk"), owners).astype(f32)
    first_grads = jnp.sum(first_grads.astype(f32), axis=0).astype(BF)
    (last,) = together([("swap", first_grads.reshape(n_u, part, -1), ("ulysses",))], 12)
    gain_sums = jnp.sum(last[:, :, head_cols : head_cols + 2].astype(f32), axis=0)
    grad_qkv = last[:, :, :head_cols].transpose(1, 0, 2).reshape(part, -1).astype(f32)
    grad_in = last_mlp[:, :, : 2 * ff_pad].reshape(n_u, part, 2, ff_pad)[..., :ff_cols]
    grad_in = grad_in.transpose(1, 2, 0, 3).reshape(part, -1).astype(f32)
    grad_down = last_mlp[:, :, 2 * ff_pad :][..., :ff_cols]
    grad_down = grad_down.transpose(1, 0, 2).reshape(part, -1).astype(f32)
    return (
        output,
        input_grad,
        gain_sums[:, 0],
        grad_qkv,
        grad_out,
        gain_sums[:, 1],
        grad_in,
        grad_down,
    )


def solution(mesh):
    in_specs = (
        P("dp", ("ulysses", "blk"), None),
        P(("dp", "ulysses", "blk")),
        P(("dp", "ulysses", "blk"), None),
        P(("dp", "ulysses", "blk"), None),
        P(("dp", "ulysses", "blk")),
        P(("dp", "ulysses", "blk"), None),
        P(("dp", "ulysses", "blk"), None),
        P("dp", ("ulysses", "blk"), None),
    )
    out_specs = (
        P("dp", ("ulysses", "blk"), None),
        P("dp", ("ulysses", "blk"), None),
        P(("dp", "ulysses", "blk")),
        P(("dp", "ulysses", "blk"), None),
        P(("dp", "ulysses", "blk"), None),
        P(("dp", "ulysses", "blk")),
        P(("dp", "ulysses", "blk"), None),
        P(("dp", "ulysses", "blk"), None),
    )
    return jax.shard_map(body, mesh=mesh, in_specs=in_specs, out_specs=out_specs, check_vma=False)
```

```python
import math

import jax
import jax.numpy as jnp
from jax import lax
from jax.experimental import pallas as pl
from jax.experimental.pallas import tpu as pltpu
from jax.sharding import PartitionSpec as P

FF = 2624
HEADS = 16
HEAD_DIM = 64


EPSILON = 1e-05
ROPE_BASE = 160000.0


def layer_norm(values, gain):
    average = jnp.mean(values, axis=-1, keepdims=True)
    centered = values - average
    variance = jnp.mean(centered * centered, axis=-1, keepdims=True)
    return centered * lax.rsqrt(variance + EPSILON) * gain


def rope_tables(positions, half_dim):
    ladder = jnp.arange(half_dim, dtype=jnp.float32)
    frequency = ROPE_BASE ** (-2.0 * ladder / (2 * half_dim))
    angles = positions[:, None] * frequency[None, :]
    return (jnp.cos(angles)[:, None, :], jnp.sin(angles)[:, None, :])


def rotate(values, cosine, sine):
    half_dim = values.shape[-1] // 2
    first_half = values[..., :half_dim]
    second_half = values[..., half_dim:]
    return jnp.concatenate(
        [first_half * cosine - second_half * sine, second_half * cosine + first_half * sine],
        axis=-1,
    )


def rotate_back(gradient, cosine, sine):
    half_dim = gradient.shape[-1] // 2
    first_half = gradient[..., :half_dim]
    second_half = gradient[..., half_dim:]
    return jnp.concatenate(
        [first_half * cosine + second_half * sine, second_half * cosine - first_half * sine],
        axis=-1,
    )


def contract_rows(left_side, right_side):
    return lax.dot_general(
        left_side, right_side, (((0,), (0,)), ((), ())), preferred_element_type=jnp.float32
    )


def contract_cols(left_side, right_side):
    return lax.dot_general(
        left_side, right_side, (((1,), (1,)), ((), ())), preferred_element_type=jnp.float32
    )


BF = jnp.bfloat16
MESH = pl.DeviceIdType.MESH


def together(ops, cid):
    n_u = lax.axis_size("ulysses")
    counts = []
    shapes = []
    for kind, x, axes in ops:
        n = n_u if kind == "line" else math.prod(lax.axis_size(a) for a in axes)
        counts.append(n)
        shape = x.shape if kind == "swap" else (n,) + x.shape
        shapes.append(jax.ShapeDtypeStruct(shape, x.dtype))
    many = len(ops)

    def kernel(*refs):
        sources, results, sems = refs[:many], refs[many : 2 * many], refs[2 * many :]
        barrier = pltpu.get_barrier_semaphore()
        plans = []
        expected = 0
        for (kind, _, axes), n in zip(ops, counts):
            if kind == "line":
                me = lax.axis_index("ulysses")
                chip, core = me // 2, lax.rem(me, 2)
                peers = [chip * 2 + (1 - core)]
                peers += [lax.rem(chip + k, n // 2) * 2 + core for k in range(1, n // 2)]
                places = [{"ulysses": peer} for peer in peers]
            else:
                me = 0
                for a in axes:
                    me = me * lax.axis_size(a) + lax.axis_index(a)
                peers = [lax.rem(me + k, n) for k in range(1, n)]
                places = []
                for peer in peers:
                    ids = {}
                    for a in reversed(axes):
                        ids[a] = lax.rem(peer, lax.axis_size(a))
                        peer = peer // lax.axis_size(a)
                    places.append(ids)
            for ids in places:
                pl.semaphore_signal(barrier, 1, device_id=ids, device_id_type=MESH)
            expected += len(places)
            plans.append((me, peers, places))
        pl.semaphore_wait(barrier, expected)

        def remote(source, target, send, recv, ids):
            copy = pltpu.make_async_remote_copy(
                src_ref=source,
                dst_ref=target,
                send_sem=send,
                recv_sem=recv,
                device_id=ids,
                device_id_type=MESH,
            )
            copy.start()
            return copy

        started, local = [], []
        for i, (kind, _, _) in enumerate(ops):
            me, peers, places = plans[i]
            source, result = sources[i], results[i]
            send, recv, own = sems[3 * i : 3 * i + 3]
            copies = []
            for j in range(len(peers)):
                part = source.at[peers[j]] if kind == "swap" else source
                copies.append(remote(part, result.at[me], send.at[j], recv.at[j], places[j]))
            started.append(copies)
            part = source.at[me] if kind == "swap" else source
            local.append(pltpu.make_async_copy(part, result.at[me], own))
            local[-1].start()
        passed = []
        for i, (kind, _, _) in enumerate(ops):
            if kind != "line":
                continue
            me, _, places = plans[i]
            chips = counts[i] // 2
            chip, core = me // 2, lax.rem(me, 2)
            send, recv, _ = sems[3 * i : 3 * i + 3]
            for k in range(1, chips):
                started[i][k].wait_recv()
                slot = results[i].at[lax.rem(chip - k + chips, chips) * 2 + core]
                at = chips + k - 1
                passed.append(remote(slot, slot, send.at[at], recv.at[at], places[0]))
        for i, (kind, _, _) in enumerate(ops):
            for j, copy in enumerate(started[i]):
                if kind == "line" and j:
                    copy.wait_send()
                else:
                    copy.wait()
            local[i].wait()
        for copy in passed:
            copy.wait()

    scratch = []
    for n in counts:
        scratch += [pltpu.SemaphoreType.DMA((n,))] * 2 + [pltpu.SemaphoreType.DMA]
    return pl.pallas_call(
        kernel,
        out_shape=shapes,
        in_specs=[pl.BlockSpec(memory_space=pl.ANY)] * many,
        out_specs=[pl.BlockSpec(memory_space=pl.ANY)] * many,
        scratch_shapes=scratch,
        compiler_params=pltpu.CompilerParams(collective_id=cid, has_side_effects=True),
    )(*[x for _, x, _ in ops])


def scatter_line(x, cid):
    n, rows, cols = x.shape
    chips = n // 2

    def kernel(x_ref, o_ref, pair, summed, land, send, recv, pass_send, pass_recv):
        me = lax.axis_index("ulysses")
        chip, core = me // 2, lax.rem(me, 2)
        partner = chip * 2 + (1 - core)
        barrier = pltpu.get_barrier_semaphore()
        pl.semaphore_signal(barrier, 1, device_id={"ulysses": partner}, device_id_type=MESH)
        for k in range(1, chips):
            peer = lax.rem(chip + k, chips) * 2 + core
            pl.semaphore_signal(barrier, 1, device_id={"ulysses": peer}, device_id_type=MESH)
        pl.semaphore_wait(barrier, chips)
        order = list(range(1, chips)) + [0]
        near, far = {}, {}
        for k in order:
            there = lax.rem(chip + k, chips)
            near[k] = pltpu.make_async_remote_copy(
                src_ref=x_ref.at[there * 2 + (1 - core)],
                dst_ref=pair.at[k],
                send_sem=pass_send.at[k],
                recv_sem=pass_recv.at[k],
                device_id={"ulysses": partner},
                device_id_type=MESH,
            )
            near[k].start()
        for k in order:
            there = lax.rem(chip + k, chips)
            near[k].wait_recv()
            total = x_ref[there * 2 + core].astype(jnp.float32) + pair[k].astype(jnp.float32)
            if k == 0:
                o_ref[...] = total
            else:
                summed[k] = total.astype(BF)
                far[k] = pltpu.make_async_remote_copy(
                    src_ref=summed.at[k],
                    dst_ref=land.at[k],
                    send_sem=send.at[k],
                    recv_sem=recv.at[k],
                    device_id={"ulysses": there * 2 + core},
                    device_id_type=MESH,
                )
                far[k].start()
        for k in range(1, chips):
            far[k].wait_recv()
            o_ref[...] += land[k].astype(jnp.float32)
        for k in order:
            near[k].wait_send()
            if k:
                far[k].wait_send()

    block = pltpu.VMEM((chips, rows, cols), BF)
    return pl.pallas_call(
        kernel,
        out_shape=jax.ShapeDtypeStruct((rows, cols), jnp.float32),
        in_specs=[pl.BlockSpec(memory_space=pltpu.VMEM)],
        out_specs=pl.BlockSpec(memory_space=pltpu.VMEM),
        scratch_shapes=[block] * 3 + [pltpu.SemaphoreType.DMA((chips,))] * 4,
        compiler_params=pltpu.CompilerParams(
            collective_id=cid, has_side_effects=True, vmem_limit_bytes=40 * 1024 * 1024
        ),
    )(x)


def pad_to(x, cols):
    return jnp.pad(x, [(0, 0)] * (x.ndim - 1) + [(0, cols - x.shape[-1])])


def body(
    tokens,
    norm_gain_attn,
    query_key_value_weight,
    attention_output_weight,
    norm_gain_mlp,
    input_projection_weight,
    down_projection_weight,
    cotangent,
):
    seq_count, local_len, width = tokens.shape
    n_dp, n_u, n_b = (lax.axis_size(a) for a in ("dp", "ulysses", "blk"))
    part = width // (n_dp * n_u * n_b)
    heads = HEADS // n_u
    head_cols = heads * 3 * HEAD_DIM
    ff_cols = FF // n_u
    ff_pad = -(-ff_cols // 128) * 128
    rows = seq_count * local_len
    length = rows * n_u
    f32 = jnp.float32

    qkv_cut = query_key_value_weight.reshape(part, n_u, head_cols).transpose(1, 0, 2)
    gains = jnp.stack([norm_gain_attn, norm_gain_mlp], axis=1)
    gains = jnp.broadcast_to(pad_to(gains, 128)[None], (n_u, part, 128))
    first_cut = jnp.concatenate([qkv_cut, gains], axis=2)
    in_cut = pad_to(input_projection_weight.reshape(part, 2, n_u, ff_cols), ff_pad)
    in_cut = in_cut.transpose(2, 0, 1, 3).reshape(n_u, part, 2 * ff_pad)
    down_cut = pad_to(down_projection_weight.reshape(part, n_u, ff_cols), ff_pad)
    mlp_cut = jnp.concatenate([in_cut, down_cut.transpose(1, 0, 2)], axis=2)

    def in_order(gathered):
        cols = gathered.shape[-1]
        gathered = gathered.reshape(n_dp, n_b, n_u, part, cols)
        return gathered.transpose(0, 2, 1, 3, 4).reshape(width, cols)

    def by_owner(grads):
        cols = grads.shape[-1]
        grads = grads.reshape(n_dp, n_u, n_b, part, cols).transpose(0, 2, 1, 3, 4)
        return grads.reshape(n_dp * n_b, n_u * part, cols)

    both, first_cut, mlp_cut = together(
        [
            ("swap", jnp.stack([tokens, cotangent], axis=1), ("blk",)),
            ("swap", first_cut, ("ulysses",)),
            ("swap", mlp_cut, ("ulysses",)),
        ],
        1,
    )
    inputs_low = both[:, 0].reshape(rows, width)
    grad_top = both[:, 1].reshape(rows, width)
    first_full, tokens_all = together(
        [
            ("copy", first_cut.reshape(n_u * part, -1), ("dp", "blk")),
            ("line", inputs_low, None),
        ],
        2,
    )
    out_full = lax.all_gather(
        attention_output_weight, ("dp", "ulysses", "blk"), axis=0, tiled=True
    )
    first_full = in_order(first_full)
    qkv_w = first_full[:, :head_cols]
    gain_attn_f = first_full[:, head_cols].astype(f32)
    gain_mlp_f = first_full[:, head_cols + 1].astype(f32)

    inputs = inputs_low.astype(f32)
    tokens_all = tokens_all.reshape(length, width)
    cot_all = lax.all_gather(grad_top, "ulysses", axis=0, tiled=True)
    normed = layer_norm(tokens_all.astype(f32), gain_attn_f).astype(BF)
    joined = jnp.dot(normed, qkv_w, preferred_element_type=f32).astype(BF)
    joined = joined.reshape(length, heads, 3 * HEAD_DIM)
    cosine, sine = rope_tables(jnp.arange(length, dtype=f32), HEAD_DIM // 2)
    queries = rotate(joined[..., :HEAD_DIM].astype(f32), cosine, sine).astype(BF)
    keys = rotate(joined[..., HEAD_DIM : 2 * HEAD_DIM].astype(f32), cosine, sine).astype(BF)
    queries, keys = queries.transpose(1, 0, 2), keys.transpose(1, 0, 2)
    values = joined[..., 2 * HEAD_DIM :].transpose(1, 0, 2)
    scale = 1.0 / math.sqrt(HEAD_DIM)

    def probs_of(queries, keys):
        scores = jnp.einsum("hqe,hke->hqk", queries, keys, preferred_element_type=f32) * scale
        exponent = jnp.exp(scores - jnp.max(scores, axis=-1, keepdims=True))
        return exponent / jnp.sum(exponent, axis=-1, keepdims=True)

    weights = probs_of(queries, keys)
    probs = weights.astype(BF)
    attended = jnp.einsum("hqk,hke->qhe", probs, values, preferred_element_type=f32)
    attended = attended.astype(BF).reshape(n_u, rows, heads * HEAD_DIM)
    (back,) = together([("swap", attended, ("ulysses",))], 5)
    back = back.transpose(1, 0, 2).reshape(rows, width)

    middle = inputs + jnp.dot(back, out_full, preferred_element_type=f32)
    normed_mlp_own = layer_norm(middle, gain_mlp_f).astype(BF)
    normed_mlp, mlp_full = together(
        [
            ("line", normed_mlp_own, None),
            ("copy", mlp_cut.reshape(n_u * part, -1), ("dp", "blk")),
        ],
        6,
    )
    normed_mlp = normed_mlp.reshape(length, width)
    mlp_full = in_order(mlp_full)
    in_w = mlp_full[:, : 2 * ff_pad]
    down_w = mlp_full[:, 2 * ff_pad :]
    hidden = jnp.dot(normed_mlp, in_w, preferred_element_type=f32)

    def gated(hidden):
        return jax.nn.gelu(hidden[:, :ff_pad], approximate=False) * hidden[:, ff_pad:]

    active, gated_pull = jax.vjp(gated, hidden)
    active = active.astype(BF)
    grad_active = jnp.dot(cot_all, down_w, preferred_element_type=f32)
    grad_hidden = gated_pull(grad_active)[0].astype(BF)
    grad_normed = contract_cols(grad_hidden, in_w).astype(BF)
    grad_normed = scatter_line(grad_normed.reshape(n_u, rows, width), 7)
    mlp_part = contract_cols(active, down_w).astype(BF)
    mlp_sum = lax.psum_scatter(mlp_part, "ulysses", scatter_dimension=0, tiled=True)
    grad_in = contract_rows(normed_mlp, grad_hidden)
    grad_down = contract_rows(cot_all, active)
    mlp_grads = jnp.concatenate([grad_in, grad_down], axis=1).astype(BF)
    mlp_grads = lax.psum_scatter(
        by_owner(mlp_grads).reshape(width, -1), ("dp", "blk"), scatter_dimension=0, tiled=True
    )

    _, norm_pull = jax.vjp(layer_norm, middle, gain_mlp_f)
    grad_middle, gain_mlp_part = norm_pull(grad_normed)
    grad_middle = grad_top.astype(f32) + grad_middle
    grad_branch = grad_middle.astype(BF)
    grad_back = contract_cols(grad_branch, out_full).astype(BF)
    grad_back = grad_back.reshape(rows, n_u, heads * HEAD_DIM).transpose(1, 0, 2)
    (grad_heads,) = together([("swap", grad_back, ("ulysses",))], 8)
    grad_heads = grad_heads.reshape(length, heads, HEAD_DIM).transpose(1, 0, 2)
    branch_all = lax.all_gather(grad_branch, "ulysses", axis=0, tiled=True)
    grad_out = contract_rows(attended.reshape(length, heads * HEAD_DIM), branch_all)
    grad_out = grad_out.astype(BF).reshape(n_dp * n_b, part, width)

    grad_values = jnp.einsum("hqk,hqe->khe", probs, grad_heads, preferred_element_type=f32)
    grad_probs = jnp.einsum("hqe,hke->hqk", grad_heads, values, preferred_element_type=f32)
    inner = jnp.sum(weights * grad_probs, axis=-1, keepdims=True)
    grad_scores = (weights * (grad_probs - inner)).astype(BF)
    grad_q = jnp.einsum("hqk,hke->qhe", grad_scores, keys, preferred_element_type=f32) * scale
    grad_k = jnp.einsum("hqk,hqe->khe", grad_scores, queries, preferred_element_type=f32) * scale
    grad_joined = jnp.concatenate(
        [rotate_back(grad_q, cosine, sine), rotate_back(grad_k, cosine, sine), grad_values],
        axis=-1,
    )
    grad_joined = grad_joined.astype(BF).reshape(length, head_cols)
    grad_first = contract_cols(grad_joined, qkv_w).astype(BF)
    grad_first = scatter_line(grad_first.reshape(n_u, rows, width), 9)
    _, first_pull = jax.vjp(layer_norm, inputs, gain_attn_f)
    grad_input, gain_attn_part = first_pull(grad_first)
    input_grad = grad_middle + grad_input
    output = middle + mlp_sum.astype(f32)
    ends = jnp.stack([output.astype(BF), input_grad.astype(BF)], axis=0)
    ends = ends.reshape(2, seq_count, local_len, width).transpose(1, 0, 2, 3)
    gain_parts = pad_to(jnp.stack([gain_attn_part, gain_mlp_part], axis=1), 128)
    first_grads = jnp.concatenate([contract_rows(normed, grad_joined), gain_parts], axis=1)
    ends, first_grads, grad_out, last_mlp = together(
        [
            ("swap", ends, ("blk",)),
            ("swap", by_owner(first_grads.astype(BF)), ("dp", "blk")),
            ("swap", grad_out, ("dp", "blk")),
            ("swap", mlp_grads.reshape(n_u, part, -1), ("ulysses",)),
        ],
        10,
    )
    output, input_grad = ends[:, 0], ends[:, 1].astype(f32)
    owners = [
        ((d * n_u + u) * n_b + b, u * n_dp * n_b + d * n_b + b)
        for d in range(n_dp)
        for u in range(n_u)
        for b in range(n_b)
    ]
    grad_out = jnp.sum(grad_out.astype(f32), axis=0).astype(BF)
    grad_out = lax.ppermute(grad_out, ("dp", "ulysses", "blk"), owners).astype(f32)
    first_grads = jnp.sum(first_grads.astype(f32), axis=0).astype(BF)
    (last,) = together([("swap", first_grads.reshape(n_u, part, -1), ("ulysses",))], 12)
    gain_sums = jnp.sum(last[:, :, head_cols : head_cols + 2].astype(f32), axis=0)
    grad_qkv = last[:, :, :head_cols].transpose(1, 0, 2).reshape(part, -1).astype(f32)
    grad_in = last_mlp[:, :, : 2 * ff_pad].reshape(n_u, part, 2, ff_pad)[..., :ff_cols]
    grad_in = grad_in.transpose(1, 2, 0, 3).reshape(part, -1).astype(f32)
    grad_down = last_mlp[:, :, 2 * ff_pad :][..., :ff_cols]
    grad_down = grad_down.transpose(1, 0, 2).reshape(part, -1).astype(f32)
    return (
        output,
        input_grad,
        gain_sums[:, 0],
        grad_qkv,
        grad_out,
        gain_sums[:, 1],
        grad_in,
        grad_down,
    )


def solution(mesh):
    in_specs = (
        P("dp", ("ulysses", "blk"), None),
        P(("dp", "ulysses", "blk")),
        P(("dp", "ulysses", "blk"), None),
        P(("dp", "ulysses", "blk"), None),
        P(("dp", "ulysses", "blk")),
        P(("dp", "ulysses", "blk"), None),
        P(("dp", "ulysses", "blk"), None),
        P("dp", ("ulysses", "blk"), None),
    )
    out_specs = (
        P("dp", ("ulysses", "blk"), None),
        P("dp", ("ulysses", "blk"), None),
        P(("dp", "ulysses", "blk")),
        P(("dp", "ulysses", "blk"), None),
        P(("dp", "ulysses", "blk"), None),
        P(("dp", "ulysses", "blk")),
        P(("dp", "ulysses", "blk"), None),
        P(("dp", "ulysses", "blk"), None),
    )
    return jax.shard_map(body, mesh=mesh, in_specs=in_specs, out_specs=out_specs, check_vma=False)
```
